32 devices in a mesh: row: 4 (over y, core), col: 8 (over z, x).
Axes of the slice: x: 2, y: 2, z: 4, core: 2. Of those that a mesh axis runs over, the one named last changes fastest.
Arguments:
- snapshots: bfloat16 [64, 384, 1024], P(None, 'row', 'col'), may hold values from -870 to 870
Outputs:
- q_blocks: float32 [64, 384, 1024], P(None, 'row', 'col')
- r_factor: float32 [64, 64], replicated
The draws below stay inside these ranges and needn't reach their ends.
All inputs are finite; a program needn't handle non-finite values.
Results may differ from the reference program's by a relative error of at most 0.0003.
Values may be sent and summed in bfloat16 or wider, within the bound.
A program may use at most 64 MiB of HBM per device.

```python
import jax
import jax.numpy as jnp
from jax import lax

SNAP = 64
HALF = 16
NROW = 384
NCOL = 1024


def draw_snapshots(key, part):
    keys = jax.random.split(jax.random.fold_in(key, 7), 4)
    position = jnp.arange(NROW, dtype=jnp.float32) / NROW
    row_scale = jnp.exp(jnp.log(3.0) * position + jax.random.uniform(keys[0], (NROW,), jnp.float32, 0.0, jnp.log(4.0)))
    col_scale = jnp.exp(jax.random.uniform(keys[1], (NCOL,), jnp.float32, 0.0, jnp.log(3.0)))
    snap_scale = jnp.exp(jax.random.uniform(keys[2], (SNAP,), jnp.float32, 0.0, jnp.log(4.0)))
    base = jnp.clip(jax.random.normal(keys[3], (SNAP, NROW, NCOL), jnp.float32), -6.0, 6.0)
    field = base * snap_scale[:, None, None] * row_scale[None, :, None] * col_scale[None, None, :]
    return field.astype(jnp.bfloat16)


def setup_inputs(seed: int = 0) -> dict:
    splits = jax.random.split(jax.random.key(seed), 2)
    snapshots = draw_snapshots(jax.random.fold_in(splits[1], 71), 0)
    return dict(snapshots=snapshots)


def gauss_taps():
    sigma = HALF / 3.0
    offsets = jnp.arange(2 * HALF + 1, dtype=jnp.float32) - HALF
    weights = jnp.exp(-offsets * offsets / (2.0 * sigma * sigma))
    return weights / jnp.sum(weights)

def smooth(plane):
    weights = gauss_taps()
    across = jnp.zeros_like(plane)
    for k in range(2 * HALF + 1):
        across = across + weights[k] * jnp.roll(plane, HALF - k, axis=1)
    result = jnp.zeros_like(plane)
    for k in range(2 * HALF + 1):
        result = result + weights[k] * jnp.roll(across, HALF - k, axis=0)
    return result

def reference(snapshots):
    filtered = lax.map(lambda plane: smooth(plane.astype(jnp.float32)), snapshots)
    flat_field = filtered.reshape(SNAP, NROW * NCOL)
    gram = jnp.dot(flat_field, flat_field.T, precision=lax.Precision.HIGHEST) / (NROW * NCOL)
    lower = jnp.linalg.cholesky(gram)
    basis = lax.linalg.triangular_solve(lower, flat_field, left_side=True, lower=True)
    return (basis.reshape(SNAP, NROW, NCOL), lower.T)
```

```python
import functools

import jax
import jax.numpy as jnp
import ml_dtypes
import numpy as np
from jax import lax
from jax.experimental import pallas as pl
from jax.experimental.pallas import tpu as pltpu
from jax.sharding import PartitionSpec as P

HALF = 16
F32, BF16 = jnp.float32, jnp.bfloat16
MESH = pl.DeviceIdType.MESH


def taps():
    sigma = HALF / 3.0
    offsets = np.arange(2 * HALF + 1, dtype=np.float64) - HALF
    weights = np.exp(-offsets * offsets / (2.0 * sigma * sigma))
    return (weights / weights.sum()).astype(np.float32)


def split_terms(values):
    high = values.astype(ml_dtypes.bfloat16)
    low = (values - high.astype(np.float32)).astype(ml_dtypes.bfloat16)
    return high, low


def band(length):
    weights = taps()
    result = np.zeros((length + 2 * HALF, length), np.float32)
    for j in range(length):
        result[j : j + 2 * HALF + 1, j] = weights
    return result


def constants(height, width):
    fold = width // HALF
    across = band(width)
    own = across[HALF : HALF + width]
    left, right = across[:HALF], across[HALF + width :]
    own_w = np.concatenate(split_terms(own), axis=0)
    strip = np.zeros((2, fold, HALF, fold, width), np.float32)
    for s in range(fold):
        strip[0, s, :, s] = left
        strip[1, s, :, s] = right
    strip_w = np.concatenate(split_terms(strip.reshape(2 * width, fold * width)), axis=0)
    pick = np.zeros((fold, width, 2, fold, HALF), np.float32)
    for s in range(fold):
        for c in range(HALF):
            pick[s, c, 0, s, c] = 1.0
            pick[s, width - HALF + c, 1, s, c] = 1.0
    pick = pick.reshape(fold * width, 2 * width).astype(ml_dtypes.bfloat16)
    high, low = split_terms(np.ascontiguousarray(band(height).T))
    rows_w = np.concatenate([high, high, low], axis=1)
    return pick, own_w, strip_w, rows_w


def split_value(value):
    high = value.astype(BF16)
    return high, (value - high.astype(F32)).astype(BF16)


def dot(a, b):
    return jnp.dot(a, b, preferred_element_type=F32)


def filter_kernel(rows, cols, x_ref, pick_hbm, own_hbm, strip_hbm, band_hbm, field_hbm, gram_ref,
                  ext, sides, packed, pick, own_w, strip_w, band_w, filtered, field, slots_r, slots_c,
                  load_sem, send_sem, recv_sem, send_r, recv_r, send_c, recv_c, out_sem):
    count, height, width = x_ref.shape
    tall = height + 2 * HALF
    fold = width // HALF
    groups = count // fold
    me_r, me_c = lax.axis_index("row"), lax.axis_index("col")
    up, down = lax.rem(me_r + rows - 1, rows), lax.rem(me_r + 1, rows)
    left, right = lax.rem(me_c + cols - 1, cols), lax.rem(me_c + 1, cols)

    body = pl.ds(HALF, height)
    loads = [
        pltpu.make_async_copy(x_ref, ext.at[:, body, :], load_sem.at[0]),
        pltpu.make_async_copy(pick_hbm, pick, load_sem.at[1]),
        pltpu.make_async_copy(own_hbm, own_w, load_sem.at[2]),
        pltpu.make_async_copy(strip_hbm, strip_w, load_sem.at[3]),
        pltpu.make_async_copy(band_hbm, band_w, load_sem.at[4]),
    ]
    for load in loads:
        load.start()

    barrier = pltpu.get_barrier_semaphore()
    friends = [(lax.rem(me_r + k, rows), me_c) for k in range(1, rows)]
    friends += [(me_r, lax.rem(me_c + k, cols)) for k in range(1, cols)]
    friends += [(up, left), (up, right), (down, left), (down, right)]
    for friend in friends:
        pl.semaphore_signal(barrier, inc=1, device_id=friend, device_id_type=MESH)

    loads[0].wait()
    loads[1].wait()

    def pack(g, carry):
        planes = [ext[g * fold + s, HALF : HALF + height, :] for s in range(fold)]
        strips = dot(jnp.concatenate(planes, axis=1), pick[...]).astype(BF16)
        packed[0, g] = strips[:, :width]
        packed[1, g] = strips[:, width:]
        return carry

    lax.fori_loop(0, groups, pack, 0)
    pl.semaphore_wait(barrier, len(friends))

    top, bottom = pl.ds(0, HALF), pl.ds(height - HALF, HALF)
    far = pl.ds(HALF + height, HALF)

    def remote(index, src, dst, device):
        return pltpu.make_async_remote_copy(
            src_ref=src, dst_ref=dst, send_sem=send_sem.at[index], recv_sem=recv_sem.at[index],
            device_id=device, device_id_type=MESH)

    copies = [
        remote(0, packed.at[0], sides.at[1, :, body, :], (me_r, left)),
        remote(1, packed.at[1], sides.at[0, :, body, :], (me_r, right)),
        remote(2, x_ref.at[:, top, :], ext.at[:, far, :], (up, me_c)),
        remote(3, x_ref.at[:, bottom, :], ext.at[:, pl.ds(0, HALF), :], (down, me_c)),
        remote(4, packed.at[0, :, top, :], sides.at[1, :, far, :], (up, left)),
        remote(5, packed.at[1, :, top, :], sides.at[0, :, far, :], (up, right)),
        remote(6, packed.at[0, :, bottom, :], sides.at[1, :, pl.ds(0, HALF), :], (down, left)),
        remote(7, packed.at[1, :, bottom, :], sides.at[0, :, pl.ds(0, HALF), :], (down, right)),
    ]
    for copy in copies:
        copy.start()
    for load in loads[2:]:
        load.wait()
    for copy in copies:
        copy.wait()

    def smooth(g, carry):
        edge = jnp.concatenate([sides[0, g], sides[1, g]], axis=1)
        edge = dot(jnp.concatenate([edge, edge], axis=1), strip_w[...])
        for s in range(0, fold, 2):
            terms = []
            for t in (s, s + 1):
                plane = ext[g * fold + t]
                across = dot(jnp.concatenate([plane, plane], axis=1), own_w[...])
                terms.append(split_value(across + edge[:, t * width : (t + 1) * width]))
            high = jnp.concatenate([terms[0][0], terms[1][0]], axis=1)
            low = jnp.concatenate([terms[0][1], terms[1][1]], axis=1)
            result = dot(band_w[:, : 2 * tall], jnp.concatenate([high, low], axis=0))
            result += dot(band_w[:, 2 * tall :], high)
            for t in (0, 1):
                start = pl.multiple_of((g * fold + s + t) * height, 8)
                filtered[pl.ds(start, height), :] = result[:, t * width : (t + 1) * width]
        return carry

    lax.fori_loop(0, groups, smooth, 0)

    def correlate(i, total):
        wide, both = [], []
        for t in range(2):
            row = 2 * i + t
            high, low = split_value(filtered[pl.ds(row, count, stride=height), :])
            pair = jnp.concatenate([high, low], axis=0)
            field[row] = pair
            wide.append(high)
            both.append(pair)
        return total + lax.dot_general(
            jnp.concatenate(wide, axis=1), jnp.concatenate(both, axis=1),
            (((1,), (1,)), ((), ())), preferred_element_type=F32)

    total = lax.fori_loop(0, height // 2, correlate, jnp.zeros((count, 2 * count), F32))
    out = pltpu.make_async_copy(field, field_hbm, out_sem)
    out.start()
    cross = total[:, count:]
    gram = total[:, :count] + (cross + cross.T)
    part = jnp.concatenate([gram[: count // 2], gram[count // 2 :]], axis=1)

    def reduce(part, size, me, slots, sends, recvs, device):
        slots[me] = part
        copies = []
        for k in range(1, size):
            copy = pltpu.make_async_remote_copy(
                src_ref=slots.at[me], dst_ref=slots.at[me], send_sem=sends.at[k], recv_sem=recvs.at[k],
                device_id=device(lax.rem(me + k, size)), device_id_type=MESH)
            copy.start()
            copies.append(copy)
        for copy in copies:
            copy.wait()
        total = slots[0]
        for k in range(1, size):
            total = total + slots[k]
        return total

    part = reduce(part, rows, me_r, slots_r, send_r, recv_r, lambda r: (r, me_c))
    part = reduce(part, cols, me_c, slots_c, send_c, recv_c, lambda c: (me_r, c))
    points = height * width * rows * cols
    gram_ref[...] = part * np.float32(1.0 / points)
    out.wait()


def factor(gram):
    size = gram.shape[0]
    row = lax.broadcasted_iota(jnp.int32, (size, 2 * size), 0)
    lane = lax.broadcasted_iota(jnp.int32, (size, 2 * size), 1)
    identity = (row == lane - size).astype(F32)
    state = jnp.concatenate([gram, jnp.zeros_like(gram)], axis=1) + identity
    done = []
    for k in range(0, size, 8):
        live = size - k
        index = lax.broadcasted_iota(jnp.int32, (live, 2 * size), 0)
        columns = [jnp.broadcast_to(state[:, k + j : k + j + 1], (live, 2 * size)) for j in range(8)]
        pivots = [state[j : j + 1, :] for j in range(8)]
        scales = []
        for j in range(8):
            pivot = columns[j][j : j + 1, :]
            inverse = 1.0 / pivot
            scaled = columns[j] * inverse
            for t in range(j + 1, 8):
                ratio = scaled[t : t + 1, :]
                columns[t] = columns[t] - columns[j] * ratio
                pivots[t] = pivots[t] - ratio * pivots[j]
            if live > 8:
                state = state - scaled * pivots[j]
            scales.append(pivots[j] * lax.rsqrt(pivot))
        done.append(jnp.concatenate(scales, axis=0))
        state = state[8:]
    done = jnp.concatenate(done, axis=0)
    keep = (lane >= size) | (lane >= row)
    return jnp.where(keep, done, 0.0)


def basis_kernel(chunk, gram_ref, field_hbm, q_hbm, r_ref, field, basis, load_sem, store_sem):
    height, _, width = field.shape
    count = r_ref.shape[0]
    load = pltpu.make_async_copy(field_hbm, field, load_sem)
    load.start()
    packed = gram_ref[...]
    gram = jnp.concatenate([packed[:, :count], packed[:, count:]], axis=0)
    both = factor(gram)
    r_ref[...] = both[:, :count]
    high, low = split_value(both[:, count:])
    twice = jnp.concatenate([high, high], axis=1)
    load.wait()
    stores = []
    for c in range(height // chunk):
        view = basis.at[c].reshape(count * chunk, width)
        for i in range(0, chunk, 2):
            row = c * chunk + i
            pair = jnp.concatenate([field[row], field[row + 1]], axis=1)
            result = dot(twice, pair) + dot(low, pair[:count])
            for t in range(2):
                view[pl.ds(i + t, count, stride=chunk), :] = result[:, t * width : (t + 1) * width]
        store = pltpu.make_async_copy(basis.at[c], q_hbm.at[:, pl.ds(c * chunk, chunk), :], store_sem.at[c])
        store.start()
        stores.append(store)
    for store in stores:
        store.wait()


def local(rows, cols, snapshots):
    count, height, width = snapshots.shape
    pick, own_w, strip_w, rows_w = constants(height, width)
    tall = height + 2 * HALF
    groups = count * HALF // width
    anywhere = pl.BlockSpec(memory_space=pl.ANY)
    vmem = pl.BlockSpec(memory_space=pltpu.VMEM)
    dma = pltpu.SemaphoreType.DMA
    half = (count // 2, 2 * count)
    field, gram = pl.pallas_call(
        functools.partial(filter_kernel, rows, cols),
        out_shape=(jax.ShapeDtypeStruct((height, 2 * count, width), BF16), jax.ShapeDtypeStruct(half, F32)),
        in_specs=[anywhere] * 5,
        out_specs=(anywhere, vmem),
        scratch_shapes=[
            pltpu.VMEM((count, tall, width), BF16),
            pltpu.VMEM((2, groups, tall, width), BF16),
            pltpu.VMEM((2, groups, height, width), BF16),
            pltpu.VMEM(pick.shape, BF16),
            pltpu.VMEM(own_w.shape, BF16),
            pltpu.VMEM(strip_w.shape, BF16),
            pltpu.VMEM(rows_w.shape, BF16),
            pltpu.VMEM((count * height, width), F32),
            pltpu.VMEM((height, 2 * count, width), BF16),
            pltpu.VMEM((rows,) + half, F32),
            pltpu.VMEM((cols,) + half, F32),
            dma((5,)), dma((8,)), dma((8,)), dma((rows,)), dma((rows,)), dma((cols,)), dma((cols,)), dma,
        ],
        compiler_params=pltpu.CompilerParams(
            collective_id=0, has_side_effects=True, vmem_limit_bytes=40 * 2**20),
    )(snapshots, jnp.asarray(pick), jnp.asarray(own_w), jnp.asarray(strip_w), jnp.asarray(rows_w))
    chunk = 24 if height % 24 == 0 else 8
    return pl.pallas_call(
        functools.partial(basis_kernel, chunk),
        out_shape=(jax.ShapeDtypeStruct(snapshots.shape, F32), jax.ShapeDtypeStruct((count, count), F32)),
        in_specs=[vmem, anywhere],
        out_specs=(anywhere, vmem),
        scratch_shapes=[
            pltpu.VMEM((height, 2 * count, width), BF16),
            pltpu.VMEM((height // chunk, count, chunk, width), F32),
            dma, dma((height // chunk,)),
        ],
        compiler_params=pltpu.CompilerParams(vmem_limit_bytes=40 * 2**20),
    )(gram, field)


def solution(mesh):
    rows, cols = mesh.shape["row"], mesh.shape["col"]
    return jax.shard_map(
        functools.partial(local, rows, cols),
        mesh=mesh,
        in_specs=(P(None, "row", "col"),),
        out_specs=(P(None, "row", "col"), P()),
        check_vma=False,
    )
```

```python
import functools

import jax
import jax.numpy as jnp
import ml_dtypes
import numpy as np
from jax import lax
from jax.experimental import pallas as pl
from jax.experimental.pallas import tpu as pltpu
from jax.sharding import PartitionSpec as P

HALF = 16
F32, BF16 = jnp.float32, jnp.bfloat16
MESH = pl.DeviceIdType.MESH


def taps():
    sigma = HALF / 3.0
    offsets = np.arange(2 * HALF + 1, dtype=np.float64) - HALF
    weights = np.exp(-offsets * offsets / (2.0 * sigma * sigma))
    return (weights / weights.sum()).astype(np.float32)


def split_terms(values):
    high = values.astype(ml_dtypes.bfloat16)
    low = (values - high.astype(np.float32)).astype(ml_dtypes.bfloat16)
    return high, low


def band(length):
    weights = taps()
    result = np.zeros((length + 2 * HALF, length), np.float32)
    for j in range(length):
        result[j : j + 2 * HALF + 1, j] = weights
    return result


def constants(height, width):
    fold = width // HALF
    across = band(width)
    joint = np.zeros((fold, 2 * width, width), np.float32)
    pick = np.zeros((fold, width, 2, fold, HALF), np.float32)
    for s in range(fold):
        joint[s, :width] = across[HALF : HALF + width]
        joint[s, width + s * HALF : width + (s + 1) * HALF] = across[:HALF]
        joint[s, width + (s ^ 1) * HALF : width + ((s ^ 1) + 1) * HALF] = across[HALF + width :]
        for c in range(HALF):
            pick[s, width - HALF + c, 0, s, c] = 1.0
            pick[s, c, 1, s ^ 1, c] = 1.0
    pick = pick.reshape(fold * width, 2 * width).astype(ml_dtypes.bfloat16)
    joint = np.concatenate(split_terms(joint), axis=2)
    rows_w = np.concatenate(split_terms(np.ascontiguousarray(band(height).T)), axis=0)
    return pick, joint, rows_w


def split_value(value):
    high = value.astype(BF16)
    return high, (value - high.astype(F32)).astype(BF16)


def dot(a, b):
    return jnp.dot(a, b, preferred_element_type=F32)


def filter_kernel(rows, cols, x_ref, pick_hbm, joint_hbm, band_hbm, field_hbm, gram_ref,
                  ext, sides, packed, pick, joint, band_w, own_h, own_l, edge_h, edge_l, filtered, field,
                  slots_r, slots_c, load_sem, send_sem, recv_sem, send_r, recv_r, send_c, recv_c, out_sem):
    count, height, width = x_ref.shape
    fold = width // HALF
    groups = count // fold
    part_groups = groups // 2
    pitch = filtered.shape[0] // count
    me_r, me_c = lax.axis_index("row"), lax.axis_index("col")
    up, down = lax.rem(me_r + rows - 1, rows), lax.rem(me_r + 1, rows)
    left, right = lax.rem(me_c + cols - 1, cols), lax.rem(me_c + 1, cols)

    body = pl.ds(HALF, height)
    loads = [
        pltpu.make_async_copy(x_ref, ext.at[:, body, :], load_sem.at[0]),
        pltpu.make_async_copy(pick_hbm, pick, load_sem.at[1]),
        pltpu.make_async_copy(band_hbm, band_w, load_sem.at[2]),
        pltpu.make_async_copy(joint_hbm, joint, load_sem.at[3]),
    ]
    for load in loads:
        load.start()

    barrier = pltpu.get_barrier_semaphore()
    friends = [(lax.rem(me_r + k, rows), me_c) for k in range(1, rows)]
    friends += [(me_r, lax.rem(me_c + k, cols)) for k in range(1, cols)]
    friends += [(up, left), (up, right), (down, left), (down, right)]
    for friend in friends:
        pl.semaphore_signal(barrier, inc=1, device_id=friend, device_id_type=MESH)

    top, bottom = pl.ds(0, HALF), pl.ds(height - HALF, HALF)
    far = pl.ds(HALF + height, HALF)

    def remote(index, src, dst, device):
        return pltpu.make_async_remote_copy(
            src_ref=src, dst_ref=dst, send_sem=send_sem.at[index], recv_sem=recv_sem.at[index],
            device_id=device, device_id_type=MESH)

    def strips(h):
        part = pl.ds(h * part_groups, part_groups)
        return [
            remote(2 * h, packed.at[0, part], sides.at[0, part, body, :], (me_r, right)),
            remote(2 * h + 1, packed.at[1, part], sides.at[1, part, body, :], (me_r, left)),
        ]

    edges = [
        remote(4, x_ref.at[:, top, :], ext.at[:, far, :], (up, me_c)),
        remote(5, x_ref.at[:, bottom, :], ext.at[:, pl.ds(0, HALF), :], (down, me_c)),
    ]
    corners = [
        remote(6, packed.at[0, :, top, :], sides.at[0, :, far, :], (up, right)),
        remote(7, packed.at[1, :, top, :], sides.at[1, :, far, :], (up, left)),
        remote(8, packed.at[0, :, bottom, :], sides.at[0, :, pl.ds(0, HALF), :], (down, right)),
        remote(9, packed.at[1, :, bottom, :], sides.at[1, :, pl.ds(0, HALF), :], (down, left)),
    ]

    def pack(h):
        planes = []
        for s in range(fold):
            first = h * part_groups * fold + s
            planes.append(jnp.concatenate(
                [ext[first + g * fold, HALF : HALF + height, :] for g in range(part_groups)], axis=0))
        chosen = dot(jnp.concatenate(planes, axis=1), pick[...]).astype(BF16)
        for g in range(part_groups):
            lines = chosen[g * height : (g + 1) * height]
            packed[0, h * part_groups + g] = lines[:, :width]
            packed[1, h * part_groups + g] = lines[:, width:]

    loads[0].wait()
    loads[1].wait()
    pack(0)
    pl.semaphore_wait(barrier, len(friends))
    for copy in strips(0) + edges:
        copy.start()
    pack(1)
    for copy in strips(1) + corners:
        copy.start()

    loads[2].wait()
    for copy in edges:
        copy.wait()

    def down_rows(pair):
        both = dot(band_w[...], pair)
        return both[:height] + both[height:]

    def own_rows(g, carry):
        start = pl.ds(pl.multiple_of(g * height, 16), height)
        for s in range(0, fold, 2):
            n = g * fold + s
            result = down_rows(jnp.concatenate([ext[n], ext[n + 1]], axis=1))
            for t in (0, 1):
                high, low = split_value(result[:, t * width : (t + 1) * width])
                own_h[s + t, start, :] = high
                own_l[s + t, start, :] = low
        return carry

    lax.fori_loop(0, groups, own_rows, 0)
    loads[3].wait()
    lane = lax.broadcasted_iota(jnp.int32, (height, width), 1)
    even = lax.rem(lane // HALF, 2) == 0

    for h in range(2):
        for copy in strips(h) + (corners if h == 0 else []):
            copy.wait()

        def edge_rows(i, carry):
            g = h * part_groups + i
            result = down_rows(jnp.concatenate([sides[0, g], sides[1, g]], axis=1))
            before, after = result[:, :width], result[:, width:]
            start = pl.ds(pl.multiple_of(g * height, 16), height)
            for t, plane in enumerate((jnp.where(even, before, after), jnp.where(even, after, before))):
                high, low = split_value(plane)
                edge_h[t, start, :] = high
                edge_l[t, start, :] = low
            return carry

        lax.fori_loop(0, part_groups, edge_rows, 0)
        block = pl.ds(h * part_groups * height, part_groups * height)

        def columns(s, carry):
            parity = lax.rem(s, 2)
            result = dot(jnp.concatenate([own_h[s, block, :], edge_h[parity, block, :]], axis=1), joint[s])
            extra = dot(jnp.concatenate([own_l[s, block, :], edge_l[parity, block, :]], axis=1),
                        joint[s, :, :width])
            result = result[:, :width] + (result[:, width:] + extra)
            for g in range(part_groups):
                start = pl.multiple_of(((h * part_groups + g) * fold + s) * pitch, 8)
                filtered[pl.ds(start, height), :] = result[g * height : (g + 1) * height]
            return carry

        lax.fori_loop(0, fold, columns, 0)

    def correlate(i, total):
        wide, both = [], []
        for t in range(2):
            row = 2 * i + t
            high, low = split_value(filtered[pl.ds(row, count, stride=pitch), :])
            pair = jnp.concatenate([high, low], axis=0)
            field[row] = pair
            wide.append(high)
            both.append(pair)
        return total + lax.dot_general(
            jnp.concatenate(wide, axis=1), jnp.concatenate(both, axis=1),
            (((1,), (1,)), ((), ())), preferred_element_type=F32)

    total = lax.fori_loop(0, height // 2, correlate, jnp.zeros((count, 2 * count), F32))
    out = pltpu.make_async_copy(field, field_hbm, out_sem)
    out.start()
    cross = total[:, count:]
    gram = total[:, :count] + (cross + cross.T)
    part = jnp.concatenate([gram[: count // 2], gram[count // 2 :]], axis=1)

    def reduce(part, size, me, slots, sends, recvs, device):
        slots[me] = part
        copies = []
        for k in range(1, size):
            copy = pltpu.make_async_remote_copy(
                src_ref=slots.at[me], dst_ref=slots.at[me], send_sem=sends.at[k], recv_sem=recvs.at[k],
                device_id=device(lax.rem(me + k, size)), device_id_type=MESH)
            copy.start()
            copies.append(copy)
        for copy in copies:
            copy.wait()
        total = slots[0]
        for k in range(1, size):
            total = total + slots[k]
        return total

    part = reduce(part, rows, me_r, slots_r, send_r, recv_r, lambda r: (r, me_c))
    part = reduce(part, cols, me_c, slots_c, send_c, recv_c, lambda c: (me_r, c))
    points = height * width * rows * cols
    gram_ref[...] = part * np.float32(1.0 / points)
    out.wait()


def factor(gram):
    size = gram.shape[0]
    row = lax.broadcasted_iota(jnp.int32, (size, 2 * size), 0)
    lane = lax.broadcasted_iota(jnp.int32, (size, 2 * size), 1)
    identity = (row == lane - size).astype(F32)
    state = jnp.concatenate([gram, jnp.zeros_like(gram)], axis=1) + identity
    done = []
    for k in range(0, size, 8):
        live = size - k
        index = lax.broadcasted_iota(jnp.int32, (live, 2 * size), 0)
        columns = [jnp.broadcast_to(state[:, k + j : k + j + 1], (live, 2 * size)) for j in range(8)]
        pivots = [state[j : j + 1, :] for j in range(8)]
        scales = []
        for j in range(8):
            pivot = columns[j][j : j + 1, :]
            inverse = 1.0 / pivot
            scaled = columns[j] * inverse
            for t in range(j + 1, 8):
                ratio = scaled[t : t + 1, :]
                columns[t] = columns[t] - columns[j] * ratio
                pivots[t] = pivots[t] - ratio * pivots[j]
            if live > 8:
                state = state - scaled * pivots[j]
            scales.append(pivots[j] * lax.rsqrt(pivot))
        done.append(jnp.concatenate(scales, axis=0))
        state = state[8:]
    done = jnp.concatenate(done, axis=0)
    keep = (lane >= size) | (lane >= row)
    return jnp.where(keep, done, 0.0)


def basis_kernel(chunk, gram_ref, field_hbm, q_hbm, r_ref, field, basis, load_sem, store_sem):
    height, _, width = field.shape
    count = r_ref.shape[0]
    load = pltpu.make_async_copy(field_hbm, field, load_sem)
    load.start()
    packed = gram_ref[...]
    gram = jnp.concatenate([packed[:, :count], packed[:, count:]], axis=0)
    both = factor(gram)
    r_ref[...] = both[:, :count]
    high, low = split_value(both[:, count:])
    twice = jnp.concatenate([high, high], axis=1)
    load.wait()
    stores = []
    for c in range(height // chunk):
        view = basis.at[c].reshape(count * chunk, width)
        for i in range(0, chunk, 2):
            row = c * chunk + i
            pair = jnp.concatenate([field[row], field[row + 1]], axis=1)
            result = dot(twice, pair) + dot(low, pair[:count])
            for t in range(2):
                view[pl.ds(i + t, count, stride=chunk), :] = result[:, t * width : (t + 1) * width]
        store = pltpu.make_async_copy(basis.at[c], q_hbm.at[:, pl.ds(c * chunk, chunk), :], store_sem.at[c])
        store.start()
        stores.append(store)
    for store in stores:
        store.wait()


def local(rows, cols, snapshots):
    count, height, width = snapshots.shape
    pick, joint, rows_w = constants(height, width)
    tall = height + 2 * HALF
    fold = width // HALF
    groups = count // fold
    pitch = height + 8 if height % 16 == 0 else height
    anywhere = pl.BlockSpec(memory_space=pl.ANY)
    hbm = pl.BlockSpec(memory_space=pltpu.HBM)
    vmem = pl.BlockSpec(memory_space=pltpu.VMEM)
    dma = pltpu.SemaphoreType.DMA
    half = (count // 2, 2 * count)
    field, gram = pl.pallas_call(
        functools.partial(filter_kernel, rows, cols),
        out_shape=(jax.ShapeDtypeStruct((height, 2 * count, width), BF16), jax.ShapeDtypeStruct(half, F32)),
        in_specs=[hbm] * 4,
        out_specs=(anywhere, vmem),
        scratch_shapes=[
            pltpu.VMEM((count, tall, width), BF16),
            pltpu.VMEM((2, groups, tall, width), BF16),
            pltpu.VMEM((2, groups, height, width), BF16),
            pltpu.VMEM(pick.shape, BF16),
            pltpu.VMEM(joint.shape, BF16),
            pltpu.VMEM(rows_w.shape, BF16),
            pltpu.VMEM((fold, groups * height, width), BF16),
            pltpu.VMEM((fold, groups * height, width), BF16),
            pltpu.VMEM((2, groups * height, width), BF16),
            pltpu.VMEM((2, groups * height, width), BF16),
            pltpu.VMEM((count * pitch, width), F32),
            pltpu.VMEM((height, 2 * count, width), BF16),
            pltpu.VMEM((rows,) + half, F32),
            pltpu.VMEM((cols,) + half, F32),
            dma((4,)), dma((10,)), dma((10,)), dma((rows,)), dma((rows,)), dma((cols,)), dma((cols,)), dma,
        ],
        compiler_params=pltpu.CompilerParams(
            collective_id=0, has_side_effects=True, vmem_limit_bytes=63 * 2**20),
    )(snapshots, jnp.asarray(pick), jnp.asarray(joint), jnp.asarray(rows_w))
    chunk = 24 if height % 24 == 0 else 8
    return pl.pallas_call(
        functools.partial(basis_kernel, chunk),
        out_shape=(jax.ShapeDtypeStruct(snapshots.shape, F32), jax.ShapeDtypeStruct((count, count), F32)),
        in_specs=[vmem, anywhere],
        out_specs=(anywhere, vmem),
        scratch_shapes=[
            pltpu.VMEM((height, 2 * count, width), BF16),
            pltpu.VMEM((height // chunk, count, chunk, width), F32),
            dma, dma((height // chunk,)),
        ],
        compiler_params=pltpu.CompilerParams(vmem_limit_bytes=63 * 2**20),
    )(gram, field)


def solution(mesh):
    rows, cols = mesh.shape["row"], mesh.shape["col"]
    return jax.shard_map(
        functools.partial(local, rows, cols),
        mesh=mesh,
        in_specs=(P(None, "row", "col"),),
        out_specs=(P(None, "row", "col"), P()),
        check_vma=False,
    )
```

```python
import functools

import jax
import jax.numpy as jnp
import ml_dtypes
import numpy as np
from jax import lax
from jax.experimental import pallas as pl
from jax.experimental.pallas import tpu as pltpu
from jax.sharding import PartitionSpec as P

HALF = 16
F32, BF16 = jnp.float32, jnp.bfloat16
MESH = pl.DeviceIdType.MESH


def taps():
    sigma = HALF / 3.0
    offsets = np.arange(2 * HALF + 1, dtype=np.float64) - HALF
    weights = np.exp(-offsets * offsets / (2.0 * sigma * sigma))
    return (weights / weights.sum()).astype(np.float32)


def split_terms(values):
    high = values.astype(ml_dtypes.bfloat16)
    low = (values - high.astype(np.float32)).astype(ml_dtypes.bfloat16)
    return high, low


def band(length):
    weights = taps()
    result = np.zeros((length + 2 * HALF, length), np.float32)
    for j in range(length):
        result[j : j + 2 * HALF + 1, j] = weights
    return result


def constants(height, width):
    fold = width // HALF
    across = band(width)
    joint = np.zeros((fold, 2 * width, width), np.float32)
    pick = np.zeros((fold, width, 2, fold, HALF), np.float32)
    for s in range(fold):
        joint[s, :width] = across[HALF : HALF + width]
        joint[s, width + s * HALF : width + (s + 1) * HALF] = across[:HALF]
        joint[s, width + (s ^ 1) * HALF : width + ((s ^ 1) + 1) * HALF] = across[HALF + width :]
        for c in range(HALF):
            pick[s, width - HALF + c, 0, s, c] = 1.0
            pick[s, c, 1, s ^ 1, c] = 1.0
    pick = pick.reshape(fold * width, 2 * width).astype(ml_dtypes.bfloat16)
    joint = np.concatenate(split_terms(joint), axis=2)
    rows_w = np.concatenate(split_terms(np.ascontiguousarray(band(height).T)), axis=0)
    return pick, joint, rows_w


def split_value(value):
    high = value.astype(BF16)
    return high, (value - high.astype(F32)).astype(BF16)


def dot(a, b):
    return jnp.dot(a, b, preferred_element_type=F32)


def filter_kernel(rows, cols, x_ref, pick_hbm, joint_hbm, band_hbm, field_hbm, gram_ref,
                  ext, sides, packed, pick, joint, band_w, own_h, own_l, edge_h, edge_l, filtered, field,
                  stage, slots_r, slots_c, gathered, load_sem, send_sem, recv_sem, send_r, recv_r, send_c, recv_c,
                  send_g, recv_g, out_sem):
    count, height, width = x_ref.shape
    fold = width // HALF
    groups = count // fold
    parts = 4 if groups % 4 == 0 else 1
    part_groups = groups // parts
    pitch = filtered.shape[0] // count
    me_r, me_c = lax.axis_index("row"), lax.axis_index("col")
    up, down = lax.rem(me_r + rows - 1, rows), lax.rem(me_r + 1, rows)
    left, right = lax.rem(me_c + cols - 1, cols), lax.rem(me_c + 1, cols)

    body = pl.ds(HALF, height)
    loads = [
        pltpu.make_async_copy(x_ref, ext.at[:, body, :], load_sem.at[0]),
        pltpu.make_async_copy(pick_hbm, pick, load_sem.at[1]),
        pltpu.make_async_copy(band_hbm, band_w, load_sem.at[2]),
        pltpu.make_async_copy(joint_hbm, joint, load_sem.at[3]),
    ]
    for load in loads[:2]:
        load.start()

    barrier = pltpu.get_barrier_semaphore()
    friends = [(lax.rem(me_r + k, rows), me_c) for k in range(1, rows)]
    friends += [(me_r, lax.rem(me_c + k, cols)) for k in range(1, cols)]
    for friend in friends:
        pl.semaphore_signal(barrier, inc=1, device_id=friend, device_id_type=MESH)

    top, bottom = pl.ds(0, HALF), pl.ds(height - HALF, HALF)
    far = pl.ds(HALF + height, HALF)

    def remote(index, src, dst, device):
        return pltpu.make_async_remote_copy(
            src_ref=src, dst_ref=dst, send_sem=send_sem.at[index], recv_sem=recv_sem.at[index],
            device_id=device, device_id_type=MESH)

    def strips(h):
        part = pl.ds(h * part_groups, part_groups)
        return [
            remote(2 * h, packed.at[0, part], sides.at[0, part, body, :], (me_r, right)),
            remote(2 * h + 1, packed.at[1, part], sides.at[1, part, body, :], (me_r, left)),
        ]

    edges = [
        remote(2 * parts, x_ref.at[:, top, :], ext.at[:, far, :], (up, me_c)),
        remote(2 * parts + 1, x_ref.at[:, bottom, :], ext.at[:, pl.ds(0, HALF), :], (down, me_c)),
    ]

    def corners(h):
        part = pl.ds(h * part_groups, part_groups)
        first = 2 * parts + 2 + 2 * h
        return [
            remote(first, sides.at[:, part, pl.ds(HALF, HALF), :], sides.at[:, part, far, :], (up, me_c)),
            remote(first + 1, sides.at[:, part, pl.ds(height, HALF), :], sides.at[:, part, pl.ds(0, HALF), :],
                   (down, me_c)),
        ]

    def pack(h):
        planes = []
        for s in range(fold):
            first = h * part_groups * fold + s
            planes.append(jnp.concatenate(
                [ext[first + g * fold, HALF : HALF + height, :] for g in range(part_groups)], axis=0))
        chosen = dot(jnp.concatenate(planes, axis=1), pick[...]).astype(BF16)
        for g in range(part_groups):
            lines = chosen[g * height : (g + 1) * height]
            packed[0, h * part_groups + g] = lines[:, :width]
            packed[1, h * part_groups + g] = lines[:, width:]

    loads[0].wait()
    loads[1].wait()
    pack(0)
    pl.semaphore_wait(barrier, len(friends))
    for copy in strips(0) + edges:
        copy.start()
    for load in loads[2:]:
        load.start()
    for h in range(1, parts):
        pack(h)
        for copy in strips(h):
            copy.start()

    loads[2].wait()
    for copy in edges:
        copy.wait()

    def down_rows(pair):
        both = dot(band_w[...], pair)
        return both[:height] + both[height:]

    def own_rows(i, carry):
        for j in range(0, 2 * fold, 2):
            g, s = 2 * i + j // fold, j % fold
            start = pl.ds(pl.multiple_of(g * height, 16), height)
            n = g * fold + s
            result = down_rows(jnp.concatenate([ext[n], ext[n + 1]], axis=1))
            for t in (0, 1):
                high, low = split_value(result[:, t * width : (t + 1) * width])
                own_h[s + t, start, :] = high
                own_l[s + t, start, :] = low
        return carry

    lax.fori_loop(0, groups // 2, own_rows, 0)
    loads[3].wait()
    lane = lax.broadcasted_iota(jnp.int32, (height, width), 1)
    even = lax.rem(lane // HALF, 2) == 0

    def finish(h):
        for copy in corners(h):
            copy.wait()
        for g in range(h * part_groups, (h + 1) * part_groups):
            result = down_rows(jnp.concatenate([sides[0, g], sides[1, g]], axis=1))
            before, after = result[:, :width], result[:, width:]
            start = pl.ds(g * height, height)
            for t, plane in enumerate((jnp.where(even, before, after), jnp.where(even, after, before))):
                high, low = split_value(plane)
                edge_h[t, start, :] = high
                edge_l[t, start, :] = low
        block = pl.ds(h * part_groups * height, part_groups * height)

        def columns(i, carry):
            for parity in range(2):
                s = 2 * i + parity
                result = dot(jnp.concatenate([own_h[s, block, :], edge_h[parity, block, :]], axis=1), joint[s])
                extra = dot(jnp.concatenate([own_l[s, block, :], edge_l[parity, block, :]], axis=1),
                            joint[s, :, :width])
                result = result[:, :width] + (result[:, width:] + extra)
                for g in range(part_groups):
                    start = pl.multiple_of(((h * part_groups + g) * fold + s) * pitch, 8)
                    filtered[pl.ds(start, height), :] = result[g * height : (g + 1) * height]
            return carry

        lax.fori_loop(0, fold // 2, columns, 0)

    for h in range(parts):
        for copy in strips(h):
            copy.wait()
        for copy in corners(h):
            copy.start()
        if h > 0:
            finish(h - 1)
    finish(parts - 1)

    step = 16 if height % 16 == 0 else 2

    def correlate(i, total):
        wide, both = [], []
        for t in range(step):
            row = step * i + t
            high, low = split_value(filtered[pl.ds(row, count, stride=pitch), :])
            pair = jnp.concatenate([high, low], axis=0)
            field[row] = pair
            wide.append(high)
            both.append(pair)
        return total + lax.dot_general(
            jnp.concatenate(wide, axis=1), jnp.concatenate(both, axis=1),
            (((1,), (1,)), ((), ())), preferred_element_type=F32)

    total = lax.fori_loop(0, height // step, correlate, jnp.zeros((count, 2 * count), F32))
    out = pltpu.make_async_copy(field, field_hbm, out_sem)
    out.start()
    cross = total[:, count:]
    gram = total[:, :count] + (cross + cross.T)
    part = jnp.concatenate([gram[: count // 2], gram[count // 2 :]], axis=1)

    def exchange(size, me, source, slots, sends, recvs, device):
        copies = []
        for k in range(1, size):
            other = lax.rem(me + k, size)
            copy = pltpu.make_async_remote_copy(
                src_ref=source(other), dst_ref=slots.at[me], send_sem=sends.at[k], recv_sem=recvs.at[k],
                device_id=device(other), device_id_type=MESH)
            copy.start()
            copies.append(copy)
        for copy in copies:
            copy.wait()

    def added(slots, size):
        total = slots[0]
        for k in range(1, size):
            total = total + slots[k]
        return total

    in_row, in_col = (lambda r: (r, me_c)), (lambda c: (me_r, c))
    scatter = stage.shape[0] == rows
    lines = stage.shape[1]
    for r in range(stage.shape[0]):
        stage[r] = part[r * lines : (r + 1) * lines]
    mine = me_r if scatter else 0
    slots_r[me_r] = stage[mine]
    exchange(rows, me_r, lambda r: stage.at[r if scatter else 0], slots_r, send_r, recv_r, in_row)
    slots_c[me_c] = added(slots_r, rows)
    exchange(cols, me_c, lambda c: slots_c.at[me_c], slots_c, send_c, recv_c, in_col)
    part = added(slots_c, cols)
    if scatter:
        gathered[me_r] = part
        exchange(rows, me_r, lambda r: gathered.at[me_r], gathered, send_g, recv_g, in_row)
        part = jnp.concatenate([gathered[r] for r in range(rows)], axis=0)
    points = height * width * rows * cols
    gram_ref[...] = part * np.float32(1.0 / points)
    out.wait()


def factor(gram):
    size = gram.shape[0]
    row = lax.broadcasted_iota(jnp.int32, (size, 2 * size), 0)
    lane = lax.broadcasted_iota(jnp.int32, (size, 2 * size), 1)
    identity = (row == lane - size).astype(F32)
    state = jnp.concatenate([gram, jnp.zeros_like(gram)], axis=1) + identity
    done = []
    for k in range(0, size, 8):
        live = size - k
        index = lax.broadcasted_iota(jnp.int32, (live, 2 * size), 0)
        columns = [jnp.broadcast_to(state[:, k + j : k + j + 1], (live, 2 * size)) for j in range(8)]
        pivots = [state[j : j + 1, :] for j in range(8)]
        scales = []
        for j in range(8):
            pivot = columns[j][j : j + 1, :]
            inverse = 1.0 / pivot
            scaled = columns[j] * inverse
            for t in range(j + 1, 8):
                ratio = scaled[t : t + 1, :]
                columns[t] = columns[t] - columns[j] * ratio
                pivots[t] = pivots[t] - ratio * pivots[j]
            if live > 8:
                state = state - scaled * pivots[j]
            scales.append(pivots[j] * lax.rsqrt(pivot))
        done.append(jnp.concatenate(scales, axis=0))
        state = state[8:]
    done = jnp.concatenate(done, axis=0)
    keep = (lane >= size) | (lane >= row)
    return jnp.where(keep, done, 0.0)


def basis_kernel(chunk, gram_ref, field_hbm, q_hbm, r_ref, field, basis, load_sem, store_sem):
    height, _, width = field.shape
    count = r_ref.shape[0]
    load = pltpu.make_async_copy(field_hbm, field, load_sem)
    load.start()
    packed = gram_ref[...]
    gram = jnp.concatenate([packed[:, :count], packed[:, count:]], axis=0)
    both = factor(gram)
    r_ref[...] = both[:, :count]
    high, low = split_value(both[:, count:])
    twice = jnp.concatenate([high, high], axis=1)
    once = jnp.concatenate([low, jnp.zeros_like(low)], axis=1)
    inverse = jnp.concatenate([twice, once], axis=0)
    load.wait()
    stores = []
    for c in range(height // chunk):
        view = basis.at[c].reshape(count * chunk, width)
        for i in range(0, chunk, 2):
            row = c * chunk + i
            pair = jnp.concatenate([field[row], field[row + 1]], axis=1)
            result = dot(inverse, pair)
            result = result[:count] + result[count:]
            for t in range(2):
                view[pl.ds(i + t, count, stride=chunk), :] = result[:, t * width : (t + 1) * width]
        store = pltpu.make_async_copy(basis.at[c], q_hbm.at[:, pl.ds(c * chunk, chunk), :], store_sem.at[c])
        store.start()
        stores.append(store)
    for store in stores:
        store.wait()


def local(rows, cols, snapshots):
    count, height, width = snapshots.shape
    pick, joint, rows_w = constants(height, width)
    tall = height + 2 * HALF
    fold = width // HALF
    groups = count // fold
    pitch = height + 8 if height % 16 == 0 else height
    anywhere = pl.BlockSpec(memory_space=pl.ANY)
    hbm = pl.BlockSpec(memory_space=pltpu.HBM)
    vmem = pl.BlockSpec(memory_space=pltpu.VMEM)
    dma = pltpu.SemaphoreType.DMA
    half = (count // 2, 2 * count)
    pieces = rows if half[0] % (8 * rows) == 0 else 1
    piece = (half[0] // pieces, half[1])
    field, gram = pl.pallas_call(
        functools.partial(filter_kernel, rows, cols),
        out_shape=(jax.ShapeDtypeStruct((height, 2 * count, width), BF16), jax.ShapeDtypeStruct(half, F32)),
        in_specs=[hbm] * 4,
        out_specs=(anywhere, vmem),
        scratch_shapes=[
            pltpu.VMEM((count, tall, width), BF16),
            pltpu.VMEM((2, groups, tall, width), BF16),
            pltpu.VMEM((2, groups, height, width), BF16),
            pltpu.VMEM(pick.shape, BF16),
            pltpu.VMEM(joint.shape, BF16),
            pltpu.VMEM(rows_w.shape, BF16),
            pltpu.VMEM((fold, groups * height, width), BF16),
            pltpu.VMEM((fold, groups * height, width), BF16),
            pltpu.VMEM((2, groups * height, width), BF16),
            pltpu.VMEM((2, groups * height, width), BF16),
            pltpu.VMEM((count * pitch, width), F32),
            pltpu.VMEM((height, 2 * count, width), BF16),
            pltpu.VMEM((pieces,) + piece, F32),
            pltpu.VMEM((rows,) + piece, F32),
            pltpu.VMEM((cols,) + piece, F32),
            pltpu.VMEM((rows,) + piece, F32),
            dma((4,)), dma((18,)), dma((18,)), dma((rows,)), dma((rows,)), dma((cols,)), dma((cols,)),
            dma((rows,)), dma((rows,)), dma,
        ],
        compiler_params=pltpu.CompilerParams(
            collective_id=0, has_side_effects=True, vmem_limit_bytes=63 * 2**20),
    )(snapshots, jnp.asarray(pick), jnp.asarray(joint), jnp.asarray(rows_w))
    chunk = 24 if height % 24 == 0 else 8
    return pl.pallas_call(
        functools.partial(basis_kernel, chunk),
        out_shape=(jax.ShapeDtypeStruct(snapshots.shape, F32), jax.ShapeDtypeStruct((count, count), F32)),
        in_specs=[vmem, anywhere],
        out_specs=(anywhere, vmem),
        scratch_shapes=[
            pltpu.VMEM((height, 2 * count, width), BF16),
            pltpu.VMEM((height // chunk, count, chunk, width), F32),
            dma, dma((height // chunk,)),
        ],
        compiler_params=pltpu.CompilerParams(vmem_limit_bytes=63 * 2**20),
    )(gram, field)


def solution(mesh):
    rows, cols = mesh.shape["row"], mesh.shape["col"]
    return jax.shard_map(
        functools.partial(local, rows, cols),
        mesh=mesh,
        in_specs=(P(None, "row", "col"),),
        out_specs=(P(None, "row", "col"), P()),
        check_vma=False,
    )
```

```python
import functools

import jax
import jax.numpy as jnp
import ml_dtypes
import numpy as np
from jax import lax
from jax.experimental import pallas as pl
from jax.experimental.pallas import tpu as pltpu
from jax.sharding import PartitionSpec as P

HALF = 16
F32, BF16 = jnp.float32, jnp.bfloat16
MESH = pl.DeviceIdType.MESH


def taps():
    sigma = HALF / 3.0
    offsets = np.arange(2 * HALF + 1, dtype=np.float64) - HALF
    weights = np.exp(-offsets * offsets / (2.0 * sigma * sigma))
    return (weights / weights.sum()).astype(np.float32)


def split_terms(values):
    high = values.astype(ml_dtypes.bfloat16)
    low = (values - high.astype(np.float32)).astype(ml_dtypes.bfloat16)
    return high, low


def band(length):
    weights = taps()
    result = np.zeros((length + 2 * HALF, length), np.float32)
    for j in range(length):
        result[j : j + 2 * HALF + 1, j] = weights
    return result


def constants(height, width):
    fold = width // HALF
    across = band(width)
    joint = np.zeros((fold, 2 * width, width), np.float32)
    pick = np.zeros((fold, width, 2, fold, HALF), np.float32)
    for s in range(fold):
        joint[s, :width] = across[HALF : HALF + width]
        joint[s, width + s * HALF : width + (s + 1) * HALF] = across[:HALF]
        joint[s, width + (s ^ 1) * HALF : width + ((s ^ 1) + 1) * HALF] = across[HALF + width :]
        for c in range(HALF):
            pick[s, width - HALF + c, 0, s, c] = 1.0
            pick[s, c, 1, s ^ 1, c] = 1.0
    pick = pick.reshape(fold * width, 2 * width).astype(ml_dtypes.bfloat16)
    joint = np.concatenate(split_terms(joint), axis=2)
    rows_w = np.concatenate(split_terms(np.ascontiguousarray(band(height).T)), axis=0)
    return pick, joint, rows_w


def split_value(value):
    high = value.astype(BF16)
    return high, (value - high.astype(F32)).astype(BF16)


def dot(a, b):
    return jnp.dot(a, b, preferred_element_type=F32)


def filter_kernel(rows, cols, x_ref, pick_hbm, joint_hbm, band_hbm, field_hbm, gram_ref,
                  ext, sides, packed, pick, joint, band_w, own_h, own_l, edge_h, edge_l, filtered, field,
                  stage, slots_r, slots_c, gathered, load_sem, send_sem, recv_sem, send_r, recv_r, send_c, recv_c,
                  send_g, recv_g, out_sem):
    count, height, width = x_ref.shape
    fold = width // HALF
    groups = count // fold
    part_groups = groups // 2
    parts = groups // 2
    pitch = filtered.shape[0] // count
    me_r, me_c = lax.axis_index("row"), lax.axis_index("col")
    up, down = lax.rem(me_r + rows - 1, rows), lax.rem(me_r + 1, rows)
    left, right = lax.rem(me_c + cols - 1, cols), lax.rem(me_c + 1, cols)

    body = pl.ds(HALF, height)
    loads = [
        pltpu.make_async_copy(x_ref, ext.at[:, body, :], load_sem.at[0]),
        pltpu.make_async_copy(pick_hbm, pick, load_sem.at[1]),
        pltpu.make_async_copy(band_hbm, band_w, load_sem.at[2]),
        pltpu.make_async_copy(joint_hbm, joint, load_sem.at[3]),
    ]
    for load in loads:
        load.start()

    barrier = pltpu.get_barrier_semaphore()
    friends = [(lax.rem(me_r + k, rows), me_c) for k in range(1, rows)]
    friends += [(me_r, lax.rem(me_c + k, cols)) for k in range(1, cols)]
    friends += [(up, left), (up, right), (down, left), (down, right)]
    for friend in friends:
        pl.semaphore_signal(barrier, inc=1, device_id=friend, device_id_type=MESH)

    top, bottom = pl.ds(0, HALF), pl.ds(height - HALF, HALF)
    far = pl.ds(HALF + height, HALF)

    def remote(index, src, dst, device):
        return pltpu.make_async_remote_copy(
            src_ref=src, dst_ref=dst, send_sem=send_sem.at[index], recv_sem=recv_sem.at[index],
            device_id=device, device_id_type=MESH)

    def strips(h):
        part = pl.ds(h * part_groups, part_groups)
        return [
            remote(2 * h, packed.at[0, part], sides.at[0, part, body, :], (me_r, right)),
            remote(2 * h + 1, packed.at[1, part], sides.at[1, part, body, :], (me_r, left)),
        ]

    def edges(i):
        part = pl.ds(i * (count // parts), count // parts)
        first = 14 + 2 * i
        return [
            remote(first, x_ref.at[part, top, :], ext.at[part, far, :], (up, me_c)),
            remote(first + 1, x_ref.at[part, bottom, :], ext.at[part, pl.ds(0, HALF), :], (down, me_c)),
        ]

    def corners(h):
        part = pl.ds(h * part_groups, part_groups)
        near = pl.ds(0, HALF)
        return [
            remote(6 + 4 * h, packed.at[0, part, top, :], sides.at[0, part, far, :], (up, right)),
            remote(7 + 4 * h, packed.at[1, part, top, :], sides.at[1, part, far, :], (up, left)),
            remote(8 + 4 * h, packed.at[0, part, bottom, :], sides.at[0, part, near, :], (down, right)),
            remote(9 + 4 * h, packed.at[1, part, bottom, :], sides.at[1, part, near, :], (down, left)),
        ]

    def pack(h):
        planes = []
        for s in range(fold):
            first = h * part_groups * fold + s
            planes.append(jnp.concatenate(
                [ext[first + g * fold, HALF : HALF + height, :] for g in range(part_groups)], axis=0))
        chosen = dot(jnp.concatenate(planes, axis=1), pick[...]).astype(BF16)
        for g in range(part_groups):
            lines = chosen[g * height : (g + 1) * height]
            packed[0, h * part_groups + g] = lines[:, :width]
            packed[1, h * part_groups + g] = lines[:, width:]

    pl.semaphore_wait(barrier, len(friends))
    for i in range(parts):
        for copy in edges(i):
            copy.start()
    loads[0].wait()
    loads[1].wait()
    for h in range(2):
        pack(h)
        for copy in strips(h) + corners(h):
            copy.start()
    loads[2].wait()

    def down_rows(pair):
        both = dot(band_w[...], pair)
        return both[:height] + both[height:]

    def own_rows(i):
        for j in range(0, 2 * fold, 2):
            g, s = 2 * i + j // fold, j % fold
            start = pl.ds(g * height, height)
            n = g * fold + s
            result = down_rows(jnp.concatenate([ext[n], ext[n + 1]], axis=1))
            for t in (0, 1):
                high, low = split_value(result[:, t * width : (t + 1) * width])
                own_h[s + t, start, :] = high
                own_l[s + t, start, :] = low

    for i in range(parts):
        for copy in edges(i):
            copy.wait()
        own_rows(i)
    loads[3].wait()
    lane = lax.broadcasted_iota(jnp.int32, (height, width), 1)
    even = lax.rem(lane // HALF, 2) == 0

    for h in range(2):
        for copy in strips(h) + corners(h):
            copy.wait()

        for g in range(h * part_groups, (h + 1) * part_groups):
            result = down_rows(jnp.concatenate([sides[0, g], sides[1, g]], axis=1))
            before, after = result[:, :width], result[:, width:]
            start = pl.ds(g * height, height)
            for t, plane in enumerate((jnp.where(even, before, after), jnp.where(even, after, before))):
                high, low = split_value(plane)
                edge_h[t, start, :] = high
                edge_l[t, start, :] = low
        block = pl.ds(h * part_groups * height, part_groups * height)

        def columns(i, carry):
            for parity in range(2):
                s = 2 * i + parity
                result = dot(jnp.concatenate([own_h[s, block, :], edge_h[parity, block, :]], axis=1), joint[s])
                extra = dot(jnp.concatenate([own_l[s, block, :], edge_l[parity, block, :]], axis=1),
                            joint[s, :, :width])
                result = result[:, :width] + (result[:, width:] + extra)
                for g in range(part_groups):
                    start = pl.multiple_of(((h * part_groups + g) * fold + s) * pitch, 8)
                    filtered[pl.ds(start, height), :] = result[g * height : (g + 1) * height]
            return carry

        lax.fori_loop(0, fold // 2, columns, 0)

    step = 16 if height % 16 == 0 else 2

    def correlate(i, total):
        wide, both = [], []
        for t in range(step):
            row = step * i + t
            high, low = split_value(filtered[pl.ds(row, count, stride=pitch), :])
            pair = jnp.concatenate([high, low], axis=0)
            field[row] = pair
            wide.append(high)
            both.append(pair)
        return total + lax.dot_general(
            jnp.concatenate(wide, axis=1), jnp.concatenate(both, axis=1),
            (((1,), (1,)), ((), ())), preferred_element_type=F32)

    total = lax.fori_loop(0, height // step, correlate, jnp.zeros((count, 2 * count), F32))
    out = pltpu.make_async_copy(field, field_hbm, out_sem)
    out.start()
    cross = total[:, count:]
    gram = total[:, :count] + (cross + cross.T)
    part = jnp.concatenate([gram[: count // 2], gram[count // 2 :]], axis=1)

    def exchange(size, me, source, slots, sends, recvs, device):
        copies = []
        for k in range(1, size):
            other = lax.rem(me + k, size)
            copy = pltpu.make_async_remote_copy(
                src_ref=source(other), dst_ref=slots.at[me], send_sem=sends.at[k], recv_sem=recvs.at[k],
                device_id=device(other), device_id_type=MESH)
            copy.start()
            copies.append(copy)
        for copy in copies:
            copy.wait()

    def added(slots, size):
        total = slots[0]
        for k in range(1, size):
            total = total + slots[k]
        return total

    in_row, in_col = (lambda r: (r, me_c)), (lambda c: (me_r, c))
    scatter = stage.shape[0] == rows
    lines = stage.shape[1]
    for r in range(stage.shape[0]):
        stage[r] = part[r * lines : (r + 1) * lines]
    mine = me_r if scatter else 0
    slots_r[me_r] = stage[mine]
    exchange(rows, me_r, lambda r: stage.at[r if scatter else 0], slots_r, send_r, recv_r, in_row)
    slots_c[me_c] = added(slots_r, rows)
    exchange(cols, me_c, lambda c: slots_c.at[me_c], slots_c, send_c, recv_c, in_col)
    part = added(slots_c, cols)
    if scatter:
        gathered[me_r] = part
        exchange(rows, me_r, lambda r: gathered.at[me_r], gathered, send_g, recv_g, in_row)
        part = jnp.concatenate([gathered[r] for r in range(rows)], axis=0)
    points = height * width * rows * cols
    gram_ref[...] = part * np.float32(1.0 / points)
    out.wait()


def factor(gram):
    size = gram.shape[0]
    row = lax.broadcasted_iota(jnp.int32, (size, 2 * size), 0)
    lane = lax.broadcasted_iota(jnp.int32, (size, 2 * size), 1)
    identity = (row == lane - size).astype(F32)
    state = jnp.concatenate([gram, jnp.zeros_like(gram)], axis=1) + identity
    done = []
    for k in range(0, size, 8):
        live = size - k
        index = lax.broadcasted_iota(jnp.int32, (live, 2 * size), 0)
        columns = [jnp.broadcast_to(state[:, k + j : k + j + 1], (live, 2 * size)) for j in range(8)]
        pivots = [state[j : j + 1, :] for j in range(8)]
        scales = []
        for j in range(8):
            pivot = columns[j][j : j + 1, :]
            inverse = 1.0 / pivot
            scaled = columns[j] * inverse
            for t in range(j + 1, 8):
                ratio = scaled[t : t + 1, :]
                columns[t] = columns[t] - columns[j] * ratio
                pivots[t] = pivots[t] - ratio * pivots[j]
            if live > 8:
                state = state - scaled * pivots[j]
            scales.append(pivots[j] * lax.rsqrt(pivot))
        done.append(jnp.concatenate(scales, axis=0))
        state = state[8:]
    done = jnp.concatenate(done, axis=0)
    keep = (lane >= size) | (lane >= row)
    return jnp.where(keep, done, 0.0)


def basis_kernel(chunk, gram_ref, field_hbm, q_hbm, r_ref, field, basis, load_sem, store_sem):
    height, _, width = field.shape
    count = r_ref.shape[0]
    load = pltpu.make_async_copy(field_hbm, field, load_sem)
    load.start()
    packed = gram_ref[...]
    gram = jnp.concatenate([packed[:, :count], packed[:, count:]], axis=0)
    both = factor(gram)
    r_ref[...] = both[:, :count]
    high, low = split_value(both[:, count:])
    twice = jnp.concatenate([high, high], axis=1)
    load.wait()
    stores = []
    for c in range(height // chunk):
        view = basis.at[c].reshape(count * chunk, width)
        for i in range(0, chunk, 2):
            row = c * chunk + i
            pair = jnp.concatenate([field[row], field[row + 1]], axis=1)
            result = dot(twice, pair) + dot(low, pair[:count])
            for t in range(2):
                view[pl.ds(i + t, count, stride=chunk), :] = result[:, t * width : (t + 1) * width]
        store = pltpu.make_async_copy(basis.at[c], q_hbm.at[:, pl.ds(c * chunk, chunk), :], store_sem.at[c])
        store.start()
        stores.append(store)
    for store in stores:
        store.wait()


def local(rows, cols, snapshots):
    count, height, width = snapshots.shape
    pick, joint, rows_w = constants(height, width)
    tall = height + 2 * HALF
    fold = width // HALF
    groups = count // fold
    pitch = height + 8 if height % 16 == 0 else height
    anywhere = pl.BlockSpec(memory_space=pl.ANY)
    hbm = pl.BlockSpec(memory_space=pltpu.HBM)
    vmem = pl.BlockSpec(memory_space=pltpu.VMEM)
    dma = pltpu.SemaphoreType.DMA
    half = (count // 2, 2 * count)
    pieces = rows if half[0] % (8 * rows) == 0 else 1
    piece = (half[0] // pieces, half[1])
    field, gram = pl.pallas_call(
        functools.partial(filter_kernel, rows, cols),
        out_shape=(jax.ShapeDtypeStruct((height, 2 * count, width), BF16), jax.ShapeDtypeStruct(half, F32)),
        in_specs=[hbm] * 4,
        out_specs=(anywhere, vmem),
        scratch_shapes=[
            pltpu.VMEM((count, tall, width), BF16),
            pltpu.VMEM((2, groups, tall, width), BF16),
            pltpu.VMEM((2, groups, height, width), BF16),
            pltpu.VMEM(pick.shape, BF16),
            pltpu.VMEM(joint.shape, BF16),
            pltpu.VMEM(rows_w.shape, BF16),
            pltpu.VMEM((fold, groups * height, width), BF16),
            pltpu.VMEM((fold, groups * height, width), BF16),
            pltpu.VMEM((2, groups * height, width), BF16),
            pltpu.VMEM((2, groups * height, width), BF16),
            pltpu.VMEM((count * pitch, width), F32),
            pltpu.VMEM((height, 2 * count, width), BF16),
            pltpu.VMEM((pieces,) + piece, F32),
            pltpu.VMEM((rows,) + piece, F32),
            pltpu.VMEM((cols,) + piece, F32),
            pltpu.VMEM((rows,) + piece, F32),
            dma((4,)), dma((14 + groups,)), dma((14 + groups,)), dma((rows,)), dma((rows,)), dma((cols,)), dma((cols,)),
            dma((rows,)), dma((rows,)), dma,
        ],
        compiler_params=pltpu.CompilerParams(
            collective_id=0, has_side_effects=True, vmem_limit_bytes=63 * 2**20),
    )(snapshots, jnp.asarray(pick), jnp.asarray(joint), jnp.asarray(rows_w))
    chunk = 24 if height % 24 == 0 else 8
    return pl.pallas_call(
        functools.partial(basis_kernel, chunk),
        out_shape=(jax.ShapeDtypeStruct(snapshots.shape, F32), jax.ShapeDtypeStruct((count, count), F32)),
        in_specs=[vmem, anywhere],
        out_specs=(anywhere, vmem),
        scratch_shapes=[
            pltpu.VMEM((height, 2 * count, width), BF16),
            pltpu.VMEM((height // chunk, count, chunk, width), F32),
            dma, dma((height // chunk,)),
        ],
        compiler_params=pltpu.CompilerParams(vmem_limit_bytes=63 * 2**20),
    )(gram, field)


def solution(mesh):
    rows, cols = mesh.shape["row"], mesh.shape["col"]
    return jax.shard_map(
        functools.partial(local, rows, cols),
        mesh=mesh,
        in_specs=(P(None, "row", "col"),),
        out_specs=(P(None, "row", "col"), P()),
        check_vma=False,
    )
```
